32 devices in a mesh: groups: 2 (over x), seq: 8 (over z, y), mp: 2 (over core).
Axes of the slice: x: 2, y: 2, z: 4, core: 2. Of those that a mesh axis runs over, the one named last changes fastest.
Arguments:
- queries: bfloat16 [8192, 4096], P(('groups', 'seq'), 'mp'), parts along dimension 0, may hold values from -6 to 6
- keys: bfloat16 [8192, 512], P(('groups', 'seq'), 'mp'), parts along dimension 0, may hold values from -6 to 6
- values: bfloat16 [8192, 512], P(('groups', 'seq'), 'mp'), parts along dimension 0, may hold values from -6 to 6
- feat_weight: bfloat16 [32, 128, 128], P('mp'), may hold values from -0.5 to 0.5
- head_gain: float32 [4096], P('mp'), may hold values from 0.1 to 1.9
- out_weight: bfloat16 [4096, 4096], P('mp'), may hold values from -0.09375 to 0.09375
Outputs:
- mixed: bfloat16 [8192, 4096], P(('groups', 'seq', 'mp')), parts along dimension 0
The draws below stay inside these ranges and needn't reach their ends.
There are 2 independent parts, one for each index of `groups`. The reference program is written for one: setup_inputs(seed, part) draws one part's arguments, and reference() takes and returns one part's arrays. A program takes and returns all parts, laid end to end along the dimension named above; an argument that names none is the same for every part. Nothing has to cross between parts.
All inputs are finite; a program needn't handle non-finite values.
Results may differ from the reference program's by a relative error of at most 0.0083.
Values sent between devices are 32-bit elements; how exact they have to be, the bound alone decides.
A program may use at most 128 MiB of HBM per device.

```python
import jax
import jax.numpy as jnp
from jax import lax

HD = 128
HEADS = 32
KVH = 4
DOUT = 4096
TOK_DEV = 512
TOKENS = 4096
N_SEQ = 8


def draw_values(key, part):
    width = KVH * HD
    half_rows = TOKENS // 2
    first_key, second_key = jax.random.split(key, 2)
    base = jax.random.truncated_normal(first_key, -5.0, 5.0, (half_rows, width), jnp.float32)
    jitter = jax.random.truncated_normal(second_key, -4.0, 4.0, (half_rows, width), jnp.float32)
    even_rows = base
    odd_rows = 0.25 * jitter - base
    paired = jnp.stack([even_rows, odd_rows], axis=1)
    return paired.reshape(TOKENS, width).astype(jnp.bfloat16)


def block_scale(stream_key, dims, shards, low, top_value):
    def one(axis_at, parts):
        heights = jax.random.uniform(jax.random.fold_in(jax.random.fold_in(stream_key, 6), axis_at), (parts,), jnp.float32, low / len(shards), top_value / len(shards))
        return jnp.repeat(jnp.exp(heights), dims[axis_at] // parts).reshape((-1,) + (1,) * (len(dims) - axis_at - 1))

    loudness = one(*shards[0])
    for cut in shards[1:]:
        loudness = loudness * one(*cut)
    return loudness


def scatter_about(own_key, shape, deviation, limit, cuts=(), held_as=jnp.bfloat16):
    array = jax.random.normal(own_key, shape, jnp.float32) * deviation
    if len(cuts) > 0:
        array = block_scale(own_key, shape, cuts, -0.22, 0.18) * array
    return jnp.clip(array, min=-limit, max=limit).astype(held_as)


def setup_inputs(seed: int = 0, part: int = 0) -> dict:
    key_of = jax.random.split(jax.random.key(seed), 7)
    part_splits = jax.random.split(jax.random.fold_in(key_of[6], part), 7)
    return {
        "queries": scatter_about(part_splits[0], (TOKENS, HEADS * HD), 1.0, 6.0, ((0, 8), (1, 2))),
        "keys": scatter_about(part_splits[1], (TOKENS, KVH * HD), 1.0, 6.0, ((0, 8), (1, 2))),
        "values": draw_values(jax.random.fold_in(jax.random.fold_in(key_of[6], part), 71), part),
        "feat_weight": scatter_about(key_of[3], (HEADS, HD, HD), HD ** -0.5, 0.5, ((0, 2),)),
        "head_gain": jnp.clip(1.0 + 0.18 * jax.random.normal(key_of[4], (HEADS * HD,), jnp.float32), 0.1, 1.9),
        "out_weight": scatter_about(key_of[5], (HEADS * HD, DOUT), (HEADS * HD) ** -0.5, 0.09375, ((0, 2),)),
    }


def feature(inputs, feat_weight):
    mapped = jnp.einsum('thd,hde->the', inputs.astype(jnp.float32), feat_weight.astype(jnp.float32))
    return (jax.nn.elu(mapped) + 1.0).astype(jnp.bfloat16)

def reference(queries, keys, values, feat_weight, head_gain, out_weight):
    group_size = HEADS // KVH
    query_blocks = queries.reshape(N_SEQ, TOK_DEV, HEADS, HD)
    key_blocks = keys.reshape(N_SEQ, TOK_DEV, KVH, HD)
    value_blocks = values.reshape(N_SEQ, TOK_DEV, KVH, HD)
    gain_heads = head_gain.reshape(HEADS, HD).astype(jnp.float32)
    causal = jnp.arange(TOK_DEV)[:, None] >= jnp.arange(TOK_DEV)[None, :]

    def one_step(prefix, items):
        query_now, key_now, value_now = items
        feat_query = feature(query_now, feat_weight).astype(jnp.float32)
        feat_key = feature(jnp.repeat(key_now, group_size, axis=1), feat_weight).astype(jnp.float32)
        value_rep = jnp.repeat(value_now, group_size, axis=1).astype(jnp.float32)
        state_now = jnp.einsum('thf,thd->hfd', feat_key, value_rep)
        inter_part = jnp.einsum('thf,hfd->thd', feat_query, prefix, precision=lax.Precision.HIGHEST)
        scores = jnp.einsum('thf,shf->hts', feat_query, feat_key)
        scores = jnp.where(causal[None], scores, 0.0).astype(jnp.bfloat16).astype(jnp.float32)
        intra_part = jnp.einsum('hts,shd->thd', scores, value_rep)
        attn = inter_part + intra_part
        normed = attn * lax.rsqrt(lax.optimization_barrier(jnp.mean(attn * attn, axis=-1, keepdims=True)) + 1e-06) * gain_heads
        return (prefix + state_now, normed.astype(jnp.bfloat16).reshape(TOK_DEV, HEADS * HD))
    start = jnp.zeros((HEADS, HD, HD), jnp.float32)
    _, normed_all = lax.scan(one_step, start, (query_blocks, key_blocks, value_blocks))
    flat = normed_all.reshape(TOKENS, HEADS * HD)
    return jnp.dot(flat, out_weight, preferred_element_type=jnp.float32).astype(jnp.bfloat16)
```

```python
import functools

import jax
import jax.numpy as jnp
from jax import lax
from jax.experimental import pallas as pl
from jax.experimental.pallas import tpu as pltpu
from jax.sharding import PartitionSpec as P

HD = 128
PAIR = 2 * HD
COLS = 512
CUTS = 1
TAIL = 2
AHEAD = 2
MORE = 2
PART = HD // CUTS
MESH = pl.DeviceIdType.MESH
NT = (((1,), (1,)), ((), ()))


def feature(mapped):
    return jnp.where(mapped > 0.0, mapped + 1.0, jnp.exp(jnp.minimum(mapped, 0.0))).astype(jnp.bfloat16)


def kernel(
    n_seq, q_hbm, k_hbm, v_hbm, fw_hbm, gain_hbm, w_hbm, out_ref,
    q_buf, k_buf, v_buf, fw_buf, gain_buf, w_buf,
    vt_buf, fk_buf, intra_buf, nrm_buf, acc,
    s_buf, peer_s, p_buf, fwd, pre_out, pfx, mp_recv,
    stage, w_far, n_out, n_in,
    q_sem, kv_sem, w_sem,
    y_send, y_recv, z_send, z_recv, b_send, b_recv, mp_send, mp_recv_sem,
    wx_send, wx_recv, n_send, n_recv,
):
    grp = lax.axis_index("groups")
    me = lax.axis_index("seq")
    mp = lax.axis_index("mp")
    layer = lax.div(me, 2)
    side = lax.rem(me, 2)
    mate = (grp, me + 1 - 2 * side, mp)
    up = (grp, me + 2, mp)
    down = (grp, me - 2, mp)
    other_mp = 1 - mp
    peer = (grp, me, other_mp)
    has_down = layer > 0
    has_up = me + 2 < n_seq
    bottom = jnp.logical_not(has_down)
    top = jnp.logical_not(has_up)
    y_out = jnp.logical_or(side == 0, has_up)
    y_in = jnp.logical_or(side == 1, has_up)
    b_out = jnp.logical_or(side == 0, has_down)
    b_in = jnp.logical_or(side == 1, has_down)
    n_pairs = q_buf.shape[0]
    rows = q_buf.shape[1]
    half = rows // 2
    n_cols = acc.shape[0]
    n_kv = k_buf.shape[1] // HD
    pairs_kv = n_pairs // n_kv
    own_pairs = n_pairs // 2
    own_heads = 2 * own_pairs
    n_parts = own_heads * CUTS
    n_head = n_pairs - TAIL
    own_at = side * own_pairs
    mate_at = own_pairs - own_at

    def k_copy():
        return pltpu.make_async_copy(k_hbm, k_buf, kv_sem.at[0])

    def v_copy():
        return pltpu.make_async_copy(v_hbm, v_buf, kv_sem.at[1])

    def fw_copy():
        return pltpu.make_async_copy(fw_hbm, fw_buf, kv_sem.at[2])

    def gain_copy():
        return pltpu.make_async_copy(gain_hbm, gain_buf, kv_sem.at[3])

    def q_copy(i):
        at = pl.multiple_of(i * PAIR, PAIR)
        return pltpu.make_async_copy(q_hbm.at[:, pl.ds(at, PAIR)], q_buf.at[i], q_sem.at[i])

    def pair_of(j):
        return lax.rem(own_at + j, n_pairs)

    def w_copy(j):
        at = pl.multiple_of(pair_of(j) * PAIR, PAIR)
        to = pl.multiple_of(j * PAIR, PAIR)
        return pltpu.make_async_copy(w_hbm.at[pl.ds(at, PAIR), :], w_buf.at[pl.ds(to, PAIR), :], w_sem.at[j])

    def remote(src, dst, send, recv, device):
        return pltpu.make_async_remote_copy(
            src_ref=src, dst_ref=dst, send_sem=send, recv_sem=recv, device_id=device, device_id_type=MESH)

    def y_copy(k):
        return remote(s_buf.at[2 * CUTS * mate_at + k], peer_s.at[k], y_send.at[k], y_recv.at[k], mate)

    def z_copy(k):
        return remote(fwd.at[k], p_buf.at[k], z_send.at[k], z_recv.at[k], up)

    def b_copy(k):
        return remote(pre_out.at[k], pfx.at[n_parts + k], b_send.at[k], b_recv.at[k], mate)

    def mp_copy(c):
        return remote(
            acc.at[c], mp_recv.at[c],
            mp_send.at[c], mp_recv_sem.at[c], peer)

    def wx_copy(t, c):
        return remote(stage.at[t, c], w_far.at[t, c], wx_send.at[t, c], wx_recv.at[t, c], peer)

    def n_copy(t):
        return remote(n_out.at[t], n_in.at[t], n_send.at[t], n_recv.at[t], peer)

    k_copy().start()
    fw_copy().start()
    v_copy().start()

    barrier = pltpu.get_barrier_semaphore()
    pl.semaphore_signal(barrier, inc=1, device_id=mate, device_id_type=MESH)
    pl.semaphore_signal(barrier, inc=1, device_id=peer, device_id_type=MESH)

    @pl.when(has_up)
    def _():
        pl.semaphore_signal(barrier, inc=1, device_id=up, device_id_type=MESH)

    @pl.when(has_down)
    def _():
        pl.semaphore_signal(barrier, inc=1, device_id=down, device_id_type=MESH)

    gain_copy().start()

    for t in range(TAIL):
        w_copy(n_head + t).start()
    for t in range(2):
        q_copy(pair_of(t)).start()

    @pl.loop(2, n_pairs)
    def _(t):
        q_copy(pair_of(t)).start()

    @pl.loop(0, n_head)
    def _(t):
        w_copy(t).start()

    @pl.when(bottom)
    def _():
        p_buf[...] = jnp.zeros_like(p_buf)

    @pl.when(jnp.logical_not(b_in))
    def _():
        pfx[n_parts:] = jnp.zeros((n_parts, PART, HD), jnp.float32)

    k_copy().wait()
    fw_copy().wait()
    v_copy().wait()

    for g in range(n_kv):
        vt_buf[g] = v_buf[:, g * HD:(g + 1) * HD].T

    def states(i):
        kv_at = pl.multiple_of(lax.div(i, pairs_kv) * HD, HD)
        weight = jnp.concatenate([fw_buf[2 * i], fw_buf[2 * i + 1]], axis=1)
        fk = feature(jnp.dot(k_buf[:, pl.ds(kv_at, HD)], weight, preferred_element_type=jnp.float32))
        fk_buf[i] = fk
        state = jnp.dot(vt_buf[lax.div(i, pairs_kv)], fk, preferred_element_type=jnp.float32)
        for d in range(2):
            s_buf[pl.ds((2 * i + d) * CUTS, CUTS)] = state[:, d * HD:(d + 1) * HD].reshape(CUTS, PART, HD)

    @pl.loop(0, n_pairs, unroll=4)
    def _(t):
        states(lax.rem(mate_at + t, n_pairs))

    cols_step = n_cols // 4
    soon = 2

    def stage_cols(u):
        for d in range(cols_step):
            c = u * cols_step + d
            cols = pl.ds(pl.multiple_of(c * COLS, COLS), COLS)
            for t in range(TAIL):
                stage[t, c] = w_buf[pl.ds((n_head + t) * PAIR, PAIR), cols].astype(jnp.float32)

    def send_cols(u):
        for d in range(cols_step):
            for t in range(TAIL):
                wx_copy(t, u * cols_step + d).start()

    for t in range(TAIL):
        w_copy(n_head + t).wait()

    @pl.loop(0, soon)
    def _(u):
        stage_cols(u)

    pl.semaphore_wait(barrier, 2 + has_up.astype(jnp.int32) + has_down.astype(jnp.int32))

    @pl.when(y_out)
    def _():
        @pl.loop(0, n_parts)
        def _(k):
            y_copy(k).start()

    @pl.loop(0, soon)
    def _(u):
        send_cols(u)

    gain_copy().wait()

    def intra(i):
        zero = jnp.zeros((HD, HD), jnp.bfloat16)
        weight = jnp.concatenate(
            [jnp.concatenate([fw_buf[2 * i], zero], axis=1),
             jnp.concatenate([zero, fw_buf[2 * i + 1]], axis=1)], axis=0)
        fq = feature(jnp.dot(q_buf[i], weight, preferred_element_type=jnp.float32))
        q_buf[i] = fq
        kv_at = pl.multiple_of(lax.div(i, pairs_kv) * HD, HD)
        values = v_buf[:, pl.ds(kv_at, HD)]
        causal = (lax.broadcasted_iota(jnp.int32, (half, half), 0)
                  >= lax.broadcasted_iota(jnp.int32, (half, half), 1))
        for j in range(2):
            lanes = slice(j * HD, (j + 1) * HD)
            fk_h = fk_buf[i, :, lanes]
            fq_h = fq[:, lanes]
            first = lax.dot_general(fq_h[:half], fk_h[:half], NT, preferred_element_type=jnp.float32)
            first = jnp.where(causal, first, 0.0).astype(jnp.bfloat16)
            intra_buf[i, :half, lanes] = jnp.dot(first, values[:half], preferred_element_type=jnp.float32)
            left = lax.dot_general(fq_h[half:], fk_h[:half], NT, preferred_element_type=jnp.float32)
            right = lax.dot_general(fq_h[half:], fk_h[half:], NT, preferred_element_type=jnp.float32)
            right = jnp.where(causal, right, 0.0)
            low = jnp.concatenate([left.astype(jnp.bfloat16), right.astype(jnp.bfloat16)], axis=1)
            intra_buf[i, half:, lanes] = jnp.dot(low, values, preferred_element_type=jnp.float32)

    def serve(k):
        @pl.when(y_in)
        def _():
            y_copy(k).wait_recv()

        @pl.when(has_down)
        def _():
            z_copy(k).wait_recv()

        @pl.when(has_up)
        def _():
            fwd[k] = p_buf[k] + s_buf[2 * CUTS * own_at + k] + peer_s[k]
            z_copy(k).start()

        @pl.when(b_out)
        def _():
            pre_out[k] = p_buf[k] + jnp.where(side == 0, s_buf[2 * CUTS * own_at + k], 0.0)
            b_copy(k).start()

        pfx[k] = p_buf[k] + jnp.where(side == 1, peer_s[k], 0.0)

    def serve_head(h):
        for d in range(CUTS):
            serve(h * CUTS + d)

    second = layer == 1
    first_due = jnp.where(bottom, 3, jnp.where(second, 7, n_pairs))
    served = n_pairs - first_due
    @pl.loop(0, n_pairs)
    def _(u):
        @pl.when(u >= first_due)
        def _():
            serve_head(u - first_due)

        i = pair_of(u)
        q_copy(i).wait()
        intra(i)
        acc[u] = jnp.zeros((half, COLS), jnp.float32)

    @pl.when(layer >= 2)
    def _():
        @pl.loop(soon, 4)
        def _(u):
            stage_cols(u)
            send_cols(u)

    theirs = pl.ds(pl.multiple_of(other_mp * half, half), half)
    mine = pl.ds(pl.multiple_of(mp * half, half), half)

    def normed(j, span):
        i = pair_of(j)
        parts = []
        for d in range(2):
            lanes = slice(d * HD, (d + 1) * HD)
            prefix = pfx[pl.ds((2 * j + d) * CUTS, CUTS)].reshape(HD, HD)
            high = prefix.astype(jnp.bfloat16)
            low = (prefix - high.astype(jnp.float32)).astype(jnp.bfloat16)
            fq_h = q_buf[i, span, lanes]
            inter = lax.dot_general(
                jnp.concatenate([fq_h, fq_h], axis=1),
                jnp.concatenate([high, low], axis=1),
                NT, preferred_element_type=jnp.float32)
            attn = inter + intra_buf[i, span, lanes]
            scale = lax.rsqrt(jnp.mean(attn * attn, axis=-1, keepdims=True) + 1e-06)
            gain = gain_buf[pl.ds(2 * i + d, 1), :]
            parts.append((attn * scale * gain).astype(jnp.bfloat16))
        return jnp.concatenate(parts, axis=1)

    def mate_prefix(j):
        for d in range(2 * CUTS):
            b_copy((2 * j - own_heads) * CUTS + d).wait_recv()

    def attend(j):
        @pl.when(jnp.logical_and(j >= own_pairs, b_in))
        def _():
            mate_prefix(j)

        w_copy(j).wait()
        at = pl.multiple_of(j * PAIR, PAIR)
        sent = normed(j, theirs)
        for c in range(n_cols):
            acc[c] += jnp.dot(
                sent, w_buf[pl.ds(at, PAIR), c * COLS:(c + 1) * COLS], preferred_element_type=jnp.float32)
        nrm_buf[:, pl.ds(at, PAIR)] = normed(j, mine)

    def attend_last(t):
        j = n_head + t

        @pl.when(b_in)
        def _():
            mate_prefix(j)

        n_out[t] = normed(j, theirs).astype(jnp.float32)
        n_copy(t).start()
        nrm_buf[:, j * PAIR:(j + 1) * PAIR] = normed(j, mine)

    @pl.loop(0, own_heads + own_pairs)
    def _(t):
        @pl.when(jnp.logical_and(t < own_heads, t >= served))
        def _():
            serve_head(t)

        @pl.when(jnp.logical_and(layer < 2, jnp.logical_and(t >= 2, t < 6 - soon)))
        def _():
            stage_cols(t - 2 + soon)
            send_cols(t - 2 + soon)

        odd = lax.rem(t, 2) == 1
        turn = lax.div(t, 2)
        inside = t < own_heads
        mid = own_heads // 2
        j_low = jnp.where(inside, turn, t - own_pairs)
        go_low = jnp.logical_or(odd, t >= own_heads)
        j_top = jnp.where(inside, jnp.where(odd, turn, own_pairs + turn - lax.div(mid, 2)), t - own_pairs + lax.div(mid, 2))
        go_top = jnp.logical_or(odd, t >= mid)
        j_bottom = t - (own_heads - 2)
        j = jnp.where(bottom, j_bottom, jnp.where(top, j_top, j_low))
        go = jnp.where(bottom, j_bottom >= 0, jnp.where(top, go_top, go_low))
        go = jnp.logical_and(go, j < n_head)

        @pl.when(go)
        def _():
            attend(j)

    @pl.loop(0, AHEAD)
    def _(c):
        mp_copy(c).start()

    @pl.loop(0, n_cols)
    def _(c):
        for t in range(TAIL):
            wx_copy(t, c).wait_send()

    total = stage.at[0]
    deep = n_head * PAIR

    def own_rows(c):
        at = pl.multiple_of(c * COLS, COLS)
        total[c] = jnp.dot(nrm_buf[:, :deep], w_buf[:deep, pl.ds(at, COLS)], preferred_element_type=jnp.float32)

    gap = n_cols // TAIL
    for t in range(TAIL):
        attend_last(t)

        if t == TAIL - 1:
            @pl.loop(AHEAD + MORE, n_cols)
            def _(c):
                mp_copy(c).start()

        @pl.loop(t * gap, (t + 1) * gap)
        def _(c):
            if t < TAIL - 1:
                @pl.when(c < MORE)
                def _():
                    mp_copy(AHEAD + c).start()

            own_rows(c)

    for t in range(TAIL):
        n_copy(t).wait_recv()

    @pl.loop(0, n_cols)
    def _(c):
        for t in range(TAIL):
            wx_copy(t, c).wait_recv()

    far = jnp.concatenate([n_in[t] for t in range(TAIL)], axis=1).astype(jnp.bfloat16)
    last = jnp.concatenate([nrm_buf[:, deep:], far], axis=1)

    @pl.loop(0, n_cols, unroll=2)
    def _(c):
        at = pl.multiple_of(c * COLS, COLS)
        weight = jnp.concatenate(
            [w_buf[deep:, pl.ds(at, COLS)]] + [w_far[t, c].astype(jnp.bfloat16) for t in range(TAIL)], axis=0)
        total[c] += jnp.dot(last, weight, preferred_element_type=jnp.float32)

    @pl.loop(0, n_cols)
    def _(c):
        mp_copy(c).wait_recv()
        at = pl.multiple_of(c * COLS, COLS)
        out_ref[:, pl.ds(at, COLS)] = (total[c] + mp_recv[c]).astype(jnp.bfloat16)

    for t in range(TAIL):
        n_copy(t).wait_send()

    @pl.loop(0, n_parts)
    def _(k):
        @pl.when(y_out)
        def _():
            y_copy(k).wait_send()

        @pl.when(b_out)
        def _():
            b_copy(k).wait_send()

        @pl.when(has_up)
        def _():
            z_copy(k).wait_send()

    @pl.loop(0, n_cols)
    def _(c):
        mp_copy(c).wait_send()


def body(n_seq, queries, keys, values, feat_weight, head_gain, out_weight):
    rows, feats = queries.shape
    heads = feat_weight.shape[0]
    n_pairs = heads // 2
    n_parts = n_pairs * CUTS
    dout = out_weight.shape[1]
    n_cols = dout // COLS
    half = rows // 2
    bf, f32 = jnp.bfloat16, jnp.float32
    gain = head_gain.reshape(heads, HD)
    dma = pltpu.SemaphoreType.DMA
    return pl.pallas_call(
        functools.partial(kernel, n_seq),
        out_shape=pltpu.VMEM((half, dout), bf),
        in_specs=[pl.BlockSpec(memory_space=pl.ANY)] * 6,
        out_specs=pl.BlockSpec(memory_space=pltpu.VMEM),
        scratch_shapes=[
            pltpu.VMEM((n_pairs, rows, PAIR), bf),
            pltpu.VMEM(keys.shape, bf),
            pltpu.VMEM(values.shape, bf),
            pltpu.VMEM(feat_weight.shape, bf),
            pltpu.VMEM((heads, HD), f32),
            pltpu.VMEM((feats, dout), bf),
            pltpu.VMEM((keys.shape[1] // HD, HD, rows), bf),
            pltpu.VMEM((n_pairs, rows, PAIR), bf),
            pltpu.VMEM((n_pairs, rows, PAIR), f32),
            pltpu.VMEM((half, feats), bf),
            pltpu.VMEM((n_cols, half, COLS), f32),
            pltpu.VMEM((2 * n_parts, PART, HD), f32),
            pltpu.VMEM((n_parts, PART, HD), f32),
            pltpu.VMEM((n_parts, PART, HD), f32),
            pltpu.VMEM((n_parts, PART, HD), f32),
            pltpu.VMEM((n_parts, PART, HD), f32),
            pltpu.VMEM((2 * n_parts, PART, HD), f32),
            pltpu.VMEM((n_cols, half, COLS), f32),
            pltpu.VMEM((TAIL, n_cols, PAIR, COLS), f32),
            pltpu.VMEM((TAIL, n_cols, PAIR, COLS), f32),
            pltpu.VMEM((TAIL, half, PAIR), f32),
            pltpu.VMEM((TAIL, half, PAIR), f32),
            dma((n_pairs,)), dma((4,)), dma((n_pairs,)),
            dma((n_parts,)), dma((n_parts,)), dma((n_parts,)), dma((n_parts,)),
            dma((n_parts,)), dma((n_parts,)),
            dma((n_cols,)), dma((n_cols,)),
            dma((TAIL, n_cols)), dma((TAIL, n_cols)), dma((TAIL,)), dma((TAIL,)),
        ],
        compiler_params=pltpu.CompilerParams(
            collective_id=0, has_side_effects=True, vmem_limit_bytes=60 * 1024 * 1024),
        cost_estimate=pl.CostEstimate(
            flops=2 * rows * feats * dout, bytes_accessed=feats * dout * 2, transcendentals=0),
    )(queries, keys, values, feat_weight, gain, out_weight)


def solution(mesh):
    return jax.shard_map(
        functools.partial(body, mesh.shape["seq"]),
        mesh=mesh,
        in_specs=(
            P(("groups", "seq"), "mp"),
            P(("groups", "seq"), "mp"),
            P(("groups", "seq"), "mp"),
            P("mp", None, None),
            P("mp"),
            P("mp", None),
        ),
        out_specs=P(("groups", "seq", "mp"), None),
        check_vma=False,
    )
```

```python
import functools

import jax
import jax.numpy as jnp
from jax import lax
from jax.experimental import pallas as pl
from jax.experimental.pallas import tpu as pltpu
from jax.sharding import PartitionSpec as P

HD = 128
PAIR = 2 * HD
COLS = 512
CUTS = 1
TAIL = 2
AHEAD = 2
MORE = 2
PART = HD // CUTS
MESH = pl.DeviceIdType.MESH
NT = (((1,), (1,)), ((), ()))


def feature(mapped):
    return jnp.where(mapped > 0.0, mapped + 1.0, jnp.exp(jnp.minimum(mapped, 0.0))).astype(jnp.bfloat16)


def kernel(
    n_seq, q_hbm, k_hbm, v_hbm, fw_hbm, gain_hbm, w_hbm, out_ref,
    q_buf, k_buf, v_buf, fw_buf, gain_buf, w_buf,
    vt_buf, fk_buf, intra_buf, nrm_buf, acc,
    s_buf, peer_s, p_buf, fwd, pre_out, pfx, mp_recv,
    stage, w_far, n_out, n_in,
    q_sem, kv_sem, w_sem,
    y_send, y_recv, z_send, z_recv, b_send, b_recv, mp_send, mp_recv_sem,
    wx_send, wx_recv, n_send, n_recv,
):
    grp = lax.axis_index("groups")
    me = lax.axis_index("seq")
    mp = lax.axis_index("mp")
    layer = lax.div(me, 2)
    side = lax.rem(me, 2)
    mate = (grp, me + 1 - 2 * side, mp)
    up = (grp, me + 2, mp)
    down = (grp, me - 2, mp)
    other_mp = 1 - mp
    peer = (grp, me, other_mp)
    has_down = layer > 0
    has_up = me + 2 < n_seq
    bottom = jnp.logical_not(has_down)
    top = jnp.logical_not(has_up)
    y_out = jnp.logical_or(side == 0, has_up)
    y_in = jnp.logical_or(side == 1, has_up)
    b_out = jnp.logical_or(side == 0, has_down)
    b_in = jnp.logical_or(side == 1, has_down)
    n_pairs = q_buf.shape[0]
    rows = q_buf.shape[1]
    half = rows // 2
    n_cols = acc.shape[0]
    n_kv = k_buf.shape[1] // HD
    pairs_kv = n_pairs // n_kv
    own_pairs = n_pairs // 2
    own_heads = 2 * own_pairs
    n_parts = own_heads * CUTS
    n_head = n_pairs - TAIL
    own_at = side * own_pairs
    mate_at = own_pairs - own_at

    def k_copy():
        return pltpu.make_async_copy(k_hbm, k_buf, kv_sem.at[0])

    def v_copy():
        return pltpu.make_async_copy(v_hbm, v_buf, kv_sem.at[1])

    def fw_copy():
        return pltpu.make_async_copy(fw_hbm, fw_buf, kv_sem.at[2])

    def gain_copy():
        return pltpu.make_async_copy(gain_hbm, gain_buf, kv_sem.at[3])

    def q_copy(i):
        at = pl.multiple_of(i * PAIR, PAIR)
        return pltpu.make_async_copy(q_hbm.at[:, pl.ds(at, PAIR)], q_buf.at[i], q_sem.at[i])

    def pair_of(j):
        return lax.rem(own_at + j, n_pairs)

    def w_copy(j):
        at = pl.multiple_of(pair_of(j) * PAIR, PAIR)
        to = pl.multiple_of(j * PAIR, PAIR)
        return pltpu.make_async_copy(w_hbm.at[pl.ds(at, PAIR), :], w_buf.at[pl.ds(to, PAIR), :], w_sem.at[j])

    def remote(src, dst, send, recv, device):
        return pltpu.make_async_remote_copy(
            src_ref=src, dst_ref=dst, send_sem=send, recv_sem=recv, device_id=device, device_id_type=MESH)

    def y_copy(k):
        return remote(s_buf.at[2 * CUTS * mate_at + k], peer_s.at[k], y_send.at[k], y_recv.at[k], mate)

    def z_copy(k):
        return remote(fwd.at[k], p_buf.at[k], z_send.at[k], z_recv.at[k], up)

    def b_copy(k):
        return remote(pre_out.at[k], pfx.at[n_parts + k], b_send.at[k], b_recv.at[k], mate)

    def mp_copy(c):
        return remote(
            acc.at[c], mp_recv.at[c],
            mp_send.at[c], mp_recv_sem.at[c], peer)

    def wx_copy(t, c):
        return remote(stage.at[t, c], w_far.at[t, c], wx_send.at[t, c], wx_recv.at[t, c], peer)

    def n_copy(t):
        return remote(n_out.at[t], n_in.at[t], n_send.at[t], n_recv.at[t], peer)

    k_copy().start()
    fw_copy().start()
    v_copy().start()

    barrier = pltpu.get_barrier_semaphore()
    pl.semaphore_signal(barrier, inc=1, device_id=mate, device_id_type=MESH)
    pl.semaphore_signal(barrier, inc=1, device_id=peer, device_id_type=MESH)

    @pl.when(has_up)
    def _():
        pl.semaphore_signal(barrier, inc=1, device_id=up, device_id_type=MESH)

    @pl.when(has_down)
    def _():
        pl.semaphore_signal(barrier, inc=1, device_id=down, device_id_type=MESH)

    gain_copy().start()

    for t in range(TAIL):
        w_copy(n_head + t).start()
    for t in range(2):
        q_copy(pair_of(t)).start()

    @pl.loop(2, n_pairs)
    def _(t):
        q_copy(pair_of(t)).start()

    @pl.loop(0, n_head)
    def _(t):
        w_copy(t).start()

    @pl.when(bottom)
    def _():
        p_buf[...] = jnp.zeros_like(p_buf)

    @pl.when(jnp.logical_not(b_in))
    def _():
        pfx[n_parts:] = jnp.zeros((n_parts, PART, HD), jnp.float32)

    k_copy().wait()
    fw_copy().wait()
    v_copy().wait()

    for g in range(n_kv):
        vt_buf[g] = v_buf[:, g * HD:(g + 1) * HD].T

    def states(i):
        kv_at = pl.multiple_of(lax.div(i, pairs_kv) * HD, HD)
        weight = jnp.concatenate([fw_buf[2 * i], fw_buf[2 * i + 1]], axis=1)
        fk = feature(jnp.dot(k_buf[:, pl.ds(kv_at, HD)], weight, preferred_element_type=jnp.float32))
        fk_buf[i] = fk
        state = jnp.dot(vt_buf[lax.div(i, pairs_kv)], fk, preferred_element_type=jnp.float32)
        for d in range(2):
            s_buf[pl.ds((2 * i + d) * CUTS, CUTS)] = state[:, d * HD:(d + 1) * HD].reshape(CUTS, PART, HD)

    @pl.loop(0, n_pairs, unroll=4)
    def _(t):
        states(lax.rem(mate_at + t, n_pairs))

    cols_step = n_cols // 4
    soon = 2

    def stage_cols(u):
        for d in range(cols_step):
            c = u * cols_step + d
            cols = pl.ds(pl.multiple_of(c * COLS, COLS), COLS)
            for t in range(TAIL):
                stage[t, c] = w_buf[pl.ds((n_head + t) * PAIR, PAIR), cols].astype(jnp.float32)

    def send_cols(u):
        for d in range(cols_step):
            for t in range(TAIL):
                wx_copy(t, u * cols_step + d).start()

    for t in range(TAIL):
        w_copy(n_head + t).wait()

    @pl.loop(0, soon)
    def _(u):
        stage_cols(u)

    pl.semaphore_wait(barrier, 2 + has_up.astype(jnp.int32) + has_down.astype(jnp.int32))

    @pl.when(y_out)
    def _():
        @pl.loop(0, n_parts)
        def _(k):
            y_copy(k).start()

    @pl.loop(0, soon)
    def _(u):
        send_cols(u)

    gain_copy().wait()

    def intra(i):
        zero = jnp.zeros((HD, HD), jnp.bfloat16)
        weight = jnp.concatenate(
            [jnp.concatenate([fw_buf[2 * i], zero], axis=1),
             jnp.concatenate([zero, fw_buf[2 * i + 1]], axis=1)], axis=0)
        fq = feature(jnp.dot(q_buf[i], weight, preferred_element_type=jnp.float32))
        q_buf[i] = fq
        kv_at = pl.multiple_of(lax.div(i, pairs_kv) * HD, HD)
        values = v_buf[:, pl.ds(kv_at, HD)]
        causal = (lax.broadcasted_iota(jnp.int32, (half, half), 0)
                  >= lax.broadcasted_iota(jnp.int32, (half, half), 1))
        for j in range(2):
            lanes = slice(j * HD, (j + 1) * HD)
            fk_h = fk_buf[i, :, lanes]
            fq_h = fq[:, lanes]
            first = lax.dot_general(fq_h[:half], fk_h[:half], NT, preferred_element_type=jnp.float32)
            first = jnp.where(causal, first, 0.0).astype(jnp.bfloat16)
            intra_buf[i, :half, lanes] = jnp.dot(first, values[:half], preferred_element_type=jnp.float32)
            left = lax.dot_general(fq_h[half:], fk_h[:half], NT, preferred_element_type=jnp.float32)
            right = lax.dot_general(fq_h[half:], fk_h[half:], NT, preferred_element_type=jnp.float32)
            right = jnp.where(causal, right, 0.0)
            low = jnp.concatenate([left.astype(jnp.bfloat16), right.astype(jnp.bfloat16)], axis=1)
            intra_buf[i, half:, lanes] = jnp.dot(low, values, preferred_element_type=jnp.float32)

    def serve(k):
        @pl.when(y_in)
        def _():
            y_copy(k).wait_recv()

        @pl.when(has_down)
        def _():
            z_copy(k).wait_recv()

        @pl.when(has_up)
        def _():
            fwd[k] = p_buf[k] + s_buf[2 * CUTS * own_at + k] + peer_s[k]
            z_copy(k).start()

        @pl.when(b_out)
        def _():
            pre_out[k] = p_buf[k] + jnp.where(side == 0, s_buf[2 * CUTS * own_at + k], 0.0)
            b_copy(k).start()

        pfx[k] = p_buf[k] + jnp.where(side == 1, peer_s[k], 0.0)

    def serve_head(h):
        for d in range(CUTS):
            serve(h * CUTS + d)

    second = layer == 1
    first_due = jnp.where(bottom, 3, jnp.where(second, 7, n_pairs))
    served = n_pairs - first_due
    @pl.loop(0, n_pairs)
    def _(u):
        @pl.when(u >= first_due)
        def _():
            serve_head(u - first_due)

        i = pair_of(u)
        q_copy(i).wait()
        intra(i)
        acc[u] = jnp.zeros((half, COLS), jnp.float32)

    @pl.when(layer >= 2)
    def _():
        @pl.loop(soon, 4)
        def _(u):
            stage_cols(u)
            send_cols(u)

    theirs = pl.ds(pl.multiple_of(other_mp * half, half), half)
    mine = pl.ds(pl.multiple_of(mp * half, half), half)

    def normed(j, span):
        i = pair_of(j)
        parts = []
        for d in range(2):
            lanes = slice(d * HD, (d + 1) * HD)
            prefix = pfx[pl.ds((2 * j + d) * CUTS, CUTS)].reshape(HD, HD)
            high = prefix.astype(jnp.bfloat16)
            low = (prefix - high.astype(jnp.float32)).astype(jnp.bfloat16)
            fq_h = q_buf[i, span, lanes]
            inter = lax.dot_general(
                jnp.concatenate([fq_h, fq_h], axis=1),
                jnp.concatenate([high, low], axis=1),
                NT, preferred_element_type=jnp.float32)
            attn = inter + intra_buf[i, span, lanes]
            scale = lax.rsqrt(jnp.mean(attn * attn, axis=-1, keepdims=True) + 1e-06)
            gain = gain_buf[pl.ds(2 * i + d, 1), :]
            parts.append((attn * scale * gain).astype(jnp.bfloat16))
        return jnp.concatenate(parts, axis=1)

    def mate_prefix(j):
        for d in range(2 * CUTS):
            b_copy((2 * j - own_heads) * CUTS + d).wait_recv()

    def attend(j):
        @pl.when(jnp.logical_and(j >= own_pairs, b_in))
        def _():
            mate_prefix(j)

        w_copy(j).wait()
        at = pl.multiple_of(j * PAIR, PAIR)
        sent = normed(j, theirs)
        for c in range(n_cols):
            acc[c] += jnp.dot(
                sent, w_buf[pl.ds(at, PAIR), c * COLS:(c + 1) * COLS], preferred_element_type=jnp.float32)
        nrm_buf[:, pl.ds(at, PAIR)] = normed(j, mine)

    def attend_last(t):
        j = n_head + t

        @pl.when(b_in)
        def _():
            mate_prefix(j)

        n_out[t] = normed(j, theirs).astype(jnp.float32)
        n_copy(t).start()
        nrm_buf[:, j * PAIR:(j + 1) * PAIR] = normed(j, mine)

    @pl.loop(0, own_heads + own_pairs)
    def _(t):
        @pl.when(jnp.logical_and(t < own_heads, t >= served))
        def _():
            serve_head(t)

        @pl.when(jnp.logical_and(layer < 2, jnp.logical_and(t >= 2, t < 6 - soon)))
        def _():
            stage_cols(t - 2 + soon)
            send_cols(t - 2 + soon)

        odd = lax.rem(t, 2) == 1
        turn = lax.div(t, 2)
        inside = t < own_heads
        mid = own_heads // 2
        j_low = jnp.where(inside, turn, t - own_pairs)
        go_low = jnp.logical_or(odd, t >= own_heads)
        j_top = jnp.where(inside, jnp.where(odd, turn, own_pairs + turn - lax.div(mid, 2)), t - own_pairs + lax.div(mid, 2))
        go_top = jnp.logical_or(odd, t >= mid)
        j_bottom = t - (own_heads - 2)
        j = jnp.where(bottom, j_bottom, jnp.where(top, j_top, j_low))
        go = jnp.where(bottom, j_bottom >= 0, jnp.where(top, go_top, go_low))
        go = jnp.logical_and(go, j < n_head)

        @pl.when(go)
        def _():
            attend(j)

    @pl.loop(0, AHEAD)
    def _(c):
        mp_copy(c).start()

    @pl.loop(0, n_cols)
    def _(c):
        for t in range(TAIL):
            wx_copy(t, c).wait_send()

    total = stage.at[0]
    deep = n_head * PAIR

    def own_rows(c):
        at = pl.multiple_of(c * COLS, COLS)
        total[c] = jnp.dot(nrm_buf[:, :deep], w_buf[:deep, pl.ds(at, COLS)], preferred_element_type=jnp.float32)

    gap = n_cols // TAIL
    for t in range(TAIL):
        attend_last(t)

        if t < TAIL - 1:
            @pl.loop(AHEAD, AHEAD + MORE)
            def _(c):
                mp_copy(c).start()

        if t == TAIL - 1:
            @pl.loop(AHEAD + MORE, n_cols)
            def _(c):
                mp_copy(c).start()

        @pl.loop(t * gap, (t + 1) * gap, unroll=4)
        def _(c):
            own_rows(c)

    for t in range(TAIL):
        n_copy(t).wait_recv()

    @pl.loop(0, n_cols)
    def _(c):
        for t in range(TAIL):
            wx_copy(t, c).wait_recv()

    far = jnp.concatenate([n_in[t] for t in range(TAIL)], axis=1).astype(jnp.bfloat16)
    last = jnp.concatenate([nrm_buf[:, deep:], far], axis=1)

    @pl.loop(0, n_cols, unroll=8)
    def _(c):
        at = pl.multiple_of(c * COLS, COLS)
        weight = jnp.concatenate(
            [w_buf[deep:, pl.ds(at, COLS)]] + [w_far[t, c].astype(jnp.bfloat16) for t in range(TAIL)], axis=0)
        total[c] += jnp.dot(last, weight, preferred_element_type=jnp.float32)

    @pl.loop(0, n_cols, unroll=2)
    def _(c):
        mp_copy(c).wait_recv()
        at = pl.multiple_of(c * COLS, COLS)
        out_ref[:, pl.ds(at, COLS)] = (total[c] + mp_recv[c]).astype(jnp.bfloat16)

    for t in range(TAIL):
        n_copy(t).wait_send()

    @pl.loop(0, n_parts)
    def _(k):
        @pl.when(y_out)
        def _():
            y_copy(k).wait_send()

        @pl.when(b_out)
        def _():
            b_copy(k).wait_send()

        @pl.when(has_up)
        def _():
            z_copy(k).wait_send()

    @pl.loop(0, n_cols)
    def _(c):
        mp_copy(c).wait_send()


def body(n_seq, queries, keys, values, feat_weight, head_gain, out_weight):
    rows, feats = queries.shape
    heads = feat_weight.shape[0]
    n_pairs = heads // 2
    n_parts = n_pairs * CUTS
    dout = out_weight.shape[1]
    n_cols = dout // COLS
    half = rows // 2
    bf, f32 = jnp.bfloat16, jnp.float32
    gain = head_gain.reshape(heads, HD)
    dma = pltpu.SemaphoreType.DMA
    return pl.pallas_call(
        functools.partial(kernel, n_seq),
        out_shape=pltpu.VMEM((half, dout), bf),
        in_specs=[pl.BlockSpec(memory_space=pl.ANY)] * 6,
        out_specs=pl.BlockSpec(memory_space=pltpu.VMEM),
        scratch_shapes=[
            pltpu.VMEM((n_pairs, rows, PAIR), bf),
            pltpu.VMEM(keys.shape, bf),
            pltpu.VMEM(values.shape, bf),
            pltpu.VMEM(feat_weight.shape, bf),
            pltpu.VMEM((heads, HD), f32),
            pltpu.VMEM((feats, dout), bf),
            pltpu.VMEM((keys.shape[1] // HD, HD, rows), bf),
            pltpu.VMEM((n_pairs, rows, PAIR), bf),
            pltpu.VMEM((n_pairs, rows, PAIR), f32),
            pltpu.VMEM((half, feats), bf),
            pltpu.VMEM((n_cols, half, COLS), f32),
            pltpu.VMEM((2 * n_parts, PART, HD), f32),
            pltpu.VMEM((n_parts, PART, HD), f32),
            pltpu.VMEM((n_parts, PART, HD), f32),
            pltpu.VMEM((n_parts, PART, HD), f32),
            pltpu.VMEM((n_parts, PART, HD), f32),
            pltpu.VMEM((2 * n_parts, PART, HD), f32),
            pltpu.VMEM((n_cols, half, COLS), f32),
            pltpu.VMEM((TAIL, n_cols, PAIR, COLS), f32),
            pltpu.VMEM((TAIL, n_cols, PAIR, COLS), f32),
            pltpu.VMEM((TAIL, half, PAIR), f32),
            pltpu.VMEM((TAIL, half, PAIR), f32),
            dma((n_pairs,)), dma((4,)), dma((n_pairs,)),
            dma((n_parts,)), dma((n_parts,)), dma((n_parts,)), dma((n_parts,)),
            dma((n_parts,)), dma((n_parts,)),
            dma((n_cols,)), dma((n_cols,)),
            dma((TAIL, n_cols)), dma((TAIL, n_cols)), dma((TAIL,)), dma((TAIL,)),
        ],
        compiler_params=pltpu.CompilerParams(
            collective_id=0, has_side_effects=True, vmem_limit_bytes=60 * 1024 * 1024),
        cost_estimate=pl.CostEstimate(
            flops=2 * rows * feats * dout, bytes_accessed=feats * dout * 2, transcendentals=0),
    )(queries, keys, values, feat_weight, gain, out_weight)


def solution(mesh):
    return jax.shard_map(
        functools.partial(body, mesh.shape["seq"]),
        mesh=mesh,
        in_specs=(
            P(("groups", "seq"), "mp"),
            P(("groups", "seq"), "mp"),
            P(("groups", "seq"), "mp"),
            P("mp", None, None),
            P("mp"),
            P("mp", None),
        ),
        out_specs=P(("groups", "seq", "mp"), None),
        check_vma=False,
    )
```

```python
import functools

import jax
import jax.numpy as jnp
from jax import lax
from jax.experimental import pallas as pl
from jax.experimental.pallas import tpu as pltpu
from jax.sharding import PartitionSpec as P

HD = 128
PAIR = 2 * HD
COLS = 512
CUTS = 1
TAIL = 2
AHEAD = 2
MORE = 2
PART = HD // CUTS
MESH = pl.DeviceIdType.MESH
NT = (((1,), (1,)), ((), ()))


def feature(mapped):
    return jnp.where(mapped > 0.0, mapped + 1.0, jnp.exp(jnp.minimum(mapped, 0.0))).astype(jnp.bfloat16)


def kernel(
    n_seq, q_hbm, k_hbm, v_hbm, fw_hbm, gain_hbm, w_hbm, out_ref,
    q_buf, k_buf, v_buf, fw_buf, gain_buf, w_buf,
    vt_buf, fk_buf, intra_buf, nrm_buf, acc,
    s_buf, peer_s, p_buf, fwd, pre_out, pfx, mp_recv,
    stage, w_far, n_out, n_in,
    q_sem, kv_sem, w_sem,
    y_send, y_recv, z_send, z_recv, b_send, b_recv, mp_send, mp_recv_sem,
    wx_send, wx_recv, n_send, n_recv,
):
    grp = lax.axis_index("groups")
    me = lax.axis_index("seq")
    mp = lax.axis_index("mp")
    layer = lax.div(me, 2)
    side = lax.rem(me, 2)
    mate = (grp, me + 1 - 2 * side, mp)
    up = (grp, me + 2, mp)
    down = (grp, me - 2, mp)
    other_mp = 1 - mp
    peer = (grp, me, other_mp)
    has_down = layer > 0
    has_up = me + 2 < n_seq
    bottom = jnp.logical_not(has_down)
    top = jnp.logical_not(has_up)
    y_out = jnp.logical_or(side == 0, has_up)
    y_in = jnp.logical_or(side == 1, has_up)
    b_out = jnp.logical_or(side == 0, has_down)
    b_in = jnp.logical_or(side == 1, has_down)
    n_pairs = q_buf.shape[0]
    rows = q_buf.shape[1]
    half = rows // 2
    n_cols = acc.shape[0]
    n_kv = k_buf.shape[1] // HD
    pairs_kv = n_pairs // n_kv
    own_pairs = n_pairs // 2
    own_heads = 2 * own_pairs
    n_parts = own_heads * CUTS
    n_head = n_pairs - TAIL
    own_at = side * own_pairs
    mate_at = own_pairs - own_at

    def k_copy():
        return pltpu.make_async_copy(k_hbm, k_buf, kv_sem.at[0])

    def v_copy():
        return pltpu.make_async_copy(v_hbm, v_buf, kv_sem.at[1])

    def fw_copy():
        return pltpu.make_async_copy(fw_hbm, fw_buf, kv_sem.at[2])

    def gain_copy():
        return pltpu.make_async_copy(gain_hbm, gain_buf, kv_sem.at[3])

    def q_copy(i):
        at = pl.multiple_of(i * PAIR, PAIR)
        return pltpu.make_async_copy(q_hbm.at[:, pl.ds(at, PAIR)], q_buf.at[i], q_sem.at[i])

    def pair_of(j):
        return lax.rem(own_at + j, n_pairs)

    def w_copy(j):
        at = pl.multiple_of(pair_of(j) * PAIR, PAIR)
        to = pl.multiple_of(j * PAIR, PAIR)
        return pltpu.make_async_copy(w_hbm.at[pl.ds(at, PAIR), :], w_buf.at[pl.ds(to, PAIR), :], w_sem.at[j])

    def remote(src, dst, send, recv, device):
        return pltpu.make_async_remote_copy(
            src_ref=src, dst_ref=dst, send_sem=send, recv_sem=recv, device_id=device, device_id_type=MESH)

    def y_copy(k):
        return remote(s_buf.at[2 * CUTS * mate_at + k], peer_s.at[k], y_send.at[k], y_recv.at[k], mate)

    def z_copy(k):
        return remote(fwd.at[k], p_buf.at[k], z_send.at[k], z_recv.at[k], up)

    def b_copy(k):
        return remote(pre_out.at[k], pfx.at[n_parts + k], b_send.at[k], b_recv.at[k], mate)

    def mp_copy(c):
        return remote(
            acc.at[c], mp_recv.at[c],
            mp_send.at[c], mp_recv_sem.at[c], peer)

    def wx_copy(t, c):
        return remote(stage.at[t, c], w_far.at[t, c], wx_send.at[t, c], wx_recv.at[t, c], peer)

    def n_copy(t):
        return remote(n_out.at[t], n_in.at[t], n_send.at[t], n_recv.at[t], peer)

    k_copy().start()
    fw_copy().start()
    v_copy().start()

    barrier = pltpu.get_barrier_semaphore()
    pl.semaphore_signal(barrier, inc=1, device_id=mate, device_id_type=MESH)
    pl.semaphore_signal(barrier, inc=1, device_id=peer, device_id_type=MESH)

    @pl.when(has_up)
    def _():
        pl.semaphore_signal(barrier, inc=1, device_id=up, device_id_type=MESH)

    @pl.when(has_down)
    def _():
        pl.semaphore_signal(barrier, inc=1, device_id=down, device_id_type=MESH)

    gain_copy().start()

    for t in range(TAIL):
        w_copy(n_head + t).start()
    for t in range(2):
        q_copy(pair_of(t)).start()

    @pl.loop(2, n_pairs)
    def _(t):
        q_copy(pair_of(t)).start()

    @pl.loop(0, n_head)
    def _(t):
        w_copy(t).start()

    @pl.when(bottom)
    def _():
        p_buf[...] = jnp.zeros_like(p_buf)

    @pl.when(jnp.logical_not(b_in))
    def _():
        pfx[n_parts:] = jnp.zeros((n_parts, PART, HD), jnp.float32)

    k_copy().wait()
    fw_copy().wait()
    v_copy().wait()

    for g in range(n_kv):
        vt_buf[g] = v_buf[:, g * HD:(g + 1) * HD].T

    def states(i):
        kv_at = pl.multiple_of(lax.div(i, pairs_kv) * HD, HD)
        weight = jnp.concatenate([fw_buf[2 * i], fw_buf[2 * i + 1]], axis=1)
        fk = feature(jnp.dot(k_buf[:, pl.ds(kv_at, HD)], weight, preferred_element_type=jnp.float32))
        fk_buf[i] = fk
        state = jnp.dot(vt_buf[lax.div(i, pairs_kv)], fk, preferred_element_type=jnp.float32)
        for d in range(2):
            s_buf[pl.ds((2 * i + d) * CUTS, CUTS)] = state[:, d * HD:(d + 1) * HD].reshape(CUTS, PART, HD)

    @pl.loop(0, n_pairs, unroll=4)
    def _(t):
        states(lax.rem(mate_at + t, n_pairs))

    cols_step = n_cols // 4
    soon = 2

    def stage_cols(u):
        for d in range(cols_step):
            c = u * cols_step + d
            cols = pl.ds(pl.multiple_of(c * COLS, COLS), COLS)
            for t in range(TAIL):
                stage[t, c] = w_buf[pl.ds((n_head + t) * PAIR, PAIR), cols].astype(jnp.float32)

    def send_cols(u):
        for d in range(cols_step):
            for t in range(TAIL):
                wx_copy(t, u * cols_step + d).start()

    for t in range(TAIL):
        w_copy(n_head + t).wait()

    @pl.loop(0, soon)
    def _(u):
        stage_cols(u)

    pl.semaphore_wait(barrier, 2 + has_up.astype(jnp.int32) + has_down.astype(jnp.int32))

    @pl.when(y_out)
    def _():
        @pl.loop(0, n_parts)
        def _(k):
            y_copy(k).start()

    @pl.loop(0, soon)
    def _(u):
        send_cols(u)

    gain_copy().wait()

    def intra(i):
        zero = jnp.zeros((HD, HD), jnp.bfloat16)
        weight = jnp.concatenate(
            [jnp.concatenate([fw_buf[2 * i], zero], axis=1),
             jnp.concatenate([zero, fw_buf[2 * i + 1]], axis=1)], axis=0)
        fq = feature(jnp.dot(q_buf[i], weight, preferred_element_type=jnp.float32))
        q_buf[i] = fq
        kv_at = pl.multiple_of(lax.div(i, pairs_kv) * HD, HD)
        values = v_buf[:, pl.ds(kv_at, HD)]
        causal = (lax.broadcasted_iota(jnp.int32, (half, half), 0)
                  >= lax.broadcasted_iota(jnp.int32, (half, half), 1))
        for j in range(2):
            lanes = slice(j * HD, (j + 1) * HD)
            fk_h = fk_buf[i, :, lanes]
            fq_h = fq[:, lanes]
            first = lax.dot_general(fq_h[:half], fk_h[:half], NT, preferred_element_type=jnp.float32)
            first = jnp.where(causal, first, 0.0).astype(jnp.bfloat16)
            intra_buf[i, :half, lanes] = jnp.dot(first, values[:half], preferred_element_type=jnp.float32)
            left = lax.dot_general(fq_h[half:], fk_h[:half], NT, preferred_element_type=jnp.float32)
            right = lax.dot_general(fq_h[half:], fk_h[half:], NT, preferred_element_type=jnp.float32)
            right = jnp.where(causal, right, 0.0)
            low = jnp.concatenate([left.astype(jnp.bfloat16), right.astype(jnp.bfloat16)], axis=1)
            intra_buf[i, half:, lanes] = jnp.dot(low, values, preferred_element_type=jnp.float32)

    def serve(k):
        @pl.when(y_in)
        def _():
            y_copy(k).wait_recv()

        @pl.when(has_down)
        def _():
            z_copy(k).wait_recv()

        @pl.when(has_up)
        def _():
            fwd[k] = p_buf[k] + s_buf[2 * CUTS * own_at + k] + peer_s[k]
            z_copy(k).start()

        @pl.when(b_out)
        def _():
            pre_out[k] = p_buf[k] + jnp.where(side == 0, s_buf[2 * CUTS * own_at + k], 0.0)
            b_copy(k).start()

        pfx[k] = p_buf[k] + jnp.where(side == 1, peer_s[k], 0.0)

    def serve_head(h):
        for d in range(CUTS):
            serve(h * CUTS + d)

    second = layer == 1
    first_due = jnp.where(bottom, 3, jnp.where(second, 7, n_pairs))
    served = n_pairs - first_due
    @pl.loop(0, n_pairs)
    def _(u):
        @pl.when(u >= first_due)
        def _():
            serve_head(u - first_due)

        i = pair_of(u)
        q_copy(i).wait()
        intra(i)
        acc[u] = jnp.zeros((half, COLS), jnp.float32)

    @pl.when(layer >= 2)
    def _():
        @pl.loop(soon, 4)
        def _(u):
            stage_cols(u)
            send_cols(u)

    theirs = pl.ds(pl.multiple_of(other_mp * half, half), half)
    mine = pl.ds(pl.multiple_of(mp * half, half), half)

    def normed(j, span):
        i = pair_of(j)
        parts = []
        for d in range(2):
            lanes = slice(d * HD, (d + 1) * HD)
            prefix = pfx[pl.ds((2 * j + d) * CUTS, CUTS)].reshape(HD, HD)
            high = prefix.astype(jnp.bfloat16)
            low = (prefix - high.astype(jnp.float32)).astype(jnp.bfloat16)
            fq_h = q_buf[i, span, lanes]
            inter = lax.dot_general(
                jnp.concatenate([fq_h, fq_h], axis=1),
                jnp.concatenate([high, low], axis=1),
                NT, preferred_element_type=jnp.float32)
            attn = inter + intra_buf[i, span, lanes]
            scale = lax.rsqrt(jnp.mean(attn * attn, axis=-1, keepdims=True) + 1e-06)
            gain = gain_buf[pl.ds(2 * i + d, 1), :]
            parts.append((attn * scale * gain).astype(jnp.bfloat16))
        return jnp.concatenate(parts, axis=1)

    def mate_prefix(j):
        for d in range(2 * CUTS):
            b_copy((2 * j - own_heads) * CUTS + d).wait_recv()

    def attend(j):
        @pl.when(jnp.logical_and(j >= own_pairs, b_in))
        def _():
            mate_prefix(j)

        w_copy(j).wait()
        at = pl.multiple_of(j * PAIR, PAIR)
        sent = normed(j, theirs)
        for c in range(n_cols):
            acc[c] += jnp.dot(
                sent, w_buf[pl.ds(at, PAIR), c * COLS:(c + 1) * COLS], preferred_element_type=jnp.float32)
        nrm_buf[:, pl.ds(at, PAIR)] = normed(j, mine)

    def attend_last(t):
        j = n_head + t

        @pl.when(b_in)
        def _():
            mate_prefix(j)

        n_out[t] = normed(j, theirs).astype(jnp.float32)
        n_copy(t).start()
        nrm_buf[:, j * PAIR:(j + 1) * PAIR] = normed(j, mine)

    @pl.loop(0, own_heads + own_pairs)
    def _(t):
        @pl.when(t == own_heads - has_down.astype(jnp.int32))
        def _():
            @pl.when(y_out)
            def _():
                @pl.loop(0, n_parts)
                def _(k):
                    y_copy(k).wait_send()

        @pl.when(jnp.logical_and(t < own_heads, t >= served))
        def _():
            serve_head(t)

        @pl.when(jnp.logical_and(layer < 2, jnp.logical_and(t >= 2, t < 6 - soon)))
        def _():
            stage_cols(t - 2 + soon)
            send_cols(t - 2 + soon)

        odd = lax.rem(t, 2) == 1
        turn = lax.div(t, 2)
        inside = t < own_heads
        mid = own_heads // 2
        j_low = jnp.where(inside, turn, t - own_pairs)
        go_low = jnp.logical_or(odd, t >= own_heads)
        j_top = jnp.where(inside, jnp.where(odd, turn, own_pairs + turn - lax.div(mid, 2)), t - own_pairs + lax.div(mid, 2))
        go_top = jnp.logical_or(odd, t >= mid)
        j_bottom = t - (own_heads - 2)
        j = jnp.where(bottom, j_bottom, jnp.where(top, j_top, j_low))
        go = jnp.where(bottom, j_bottom >= 0, jnp.where(top, go_top, go_low))
        go = jnp.logical_and(go, j < n_head)

        @pl.when(go)
        def _():
            attend(j)

    @pl.loop(0, AHEAD)
    def _(c):
        mp_copy(c).start()

    @pl.loop(0, n_cols)
    def _(c):
        for t in range(TAIL):
            wx_copy(t, c).wait_send()
            wx_copy(t, c).wait_recv()

    total = stage.at[0]
    deep = n_head * PAIR

    def own_rows(c):
        at = pl.multiple_of(c * COLS, COLS)
        total[c] = jnp.dot(nrm_buf[:, :deep], w_buf[:deep, pl.ds(at, COLS)], preferred_element_type=jnp.float32)

    gap = n_cols // TAIL
    for t in range(TAIL):
        attend_last(t)

        if t < TAIL - 1:
            @pl.loop(AHEAD, AHEAD + MORE)
            def _(c):
                mp_copy(c).start()

        if t == TAIL - 1:
            @pl.loop(AHEAD + MORE, n_cols)
            def _(c):
                mp_copy(c).start()

        @pl.loop(t * gap, (t + 1) * gap, unroll=4)
        def _(c):
            own_rows(c)

    for t in range(TAIL):
        n_copy(t).wait_recv()

    far = jnp.concatenate([n_in[t] for t in range(TAIL)], axis=1).astype(jnp.bfloat16)
    last = jnp.concatenate([nrm_buf[:, deep:], far], axis=1)

    @pl.loop(0, n_cols, unroll=8)
    def _(c):
        at = pl.multiple_of(c * COLS, COLS)
        weight = jnp.concatenate(
            [w_buf[deep:, pl.ds(at, COLS)]] + [w_far[t, c].astype(jnp.bfloat16) for t in range(TAIL)], axis=0)
        total[c] += jnp.dot(last, weight, preferred_element_type=jnp.float32)

    for t in range(TAIL):
        n_copy(t).wait_send()

    @pl.loop(0, n_parts)
    def _(k):
        @pl.when(b_out)
        def _():
            b_copy(k).wait_send()

        @pl.when(has_up)
        def _():
            z_copy(k).wait_send()

    @pl.loop(0, n_cols, unroll=4)
    def _(c):
        mp_copy(c).wait_recv()
        at = pl.multiple_of(c * COLS, COLS)
        out_ref[:, pl.ds(at, COLS)] = (total[c] + mp_recv[c]).astype(jnp.bfloat16)

    @pl.loop(0, n_cols)
    def _(c):
        mp_copy(c).wait_send()


def body(n_seq, queries, keys, values, feat_weight, head_gain, out_weight):
    rows, feats = queries.shape
    heads = feat_weight.shape[0]
    n_pairs = heads // 2
    n_parts = n_pairs * CUTS
    dout = out_weight.shape[1]
    n_cols = dout // COLS
    half = rows // 2
    bf, f32 = jnp.bfloat16, jnp.float32
    gain = head_gain.reshape(heads, HD)
    dma = pltpu.SemaphoreType.DMA
    return pl.pallas_call(
        functools.partial(kernel, n_seq),
        out_shape=pltpu.VMEM((half, dout), bf),
        in_specs=[pl.BlockSpec(memory_space=pl.ANY)] * 6,
        out_specs=pl.BlockSpec(memory_space=pltpu.VMEM),
        scratch_shapes=[
            pltpu.VMEM((n_pairs, rows, PAIR), bf),
            pltpu.VMEM(keys.shape, bf),
            pltpu.VMEM(values.shape, bf),
            pltpu.VMEM(feat_weight.shape, bf),
            pltpu.VMEM((heads, HD), f32),
            pltpu.VMEM((feats, dout), bf),
            pltpu.VMEM((keys.shape[1] // HD, HD, rows), bf),
            pltpu.VMEM((n_pairs, rows, PAIR), bf),
            pltpu.VMEM((n_pairs, rows, PAIR), f32),
            pltpu.VMEM((half, feats), bf),
            pltpu.VMEM((n_cols, half, COLS), f32),
            pltpu.VMEM((2 * n_parts, PART, HD), f32),
            pltpu.VMEM((n_parts, PART, HD), f32),
            pltpu.VMEM((n_parts, PART, HD), f32),
            pltpu.VMEM((n_parts, PART, HD), f32),
            pltpu.VMEM((n_parts, PART, HD), f32),
            pltpu.VMEM((2 * n_parts, PART, HD), f32),
            pltpu.VMEM((n_cols, half, COLS), f32),
            pltpu.VMEM((TAIL, n_cols, PAIR, COLS), f32),
            pltpu.VMEM((TAIL, n_cols, PAIR, COLS), f32),
            pltpu.VMEM((TAIL, half, PAIR), f32),
            pltpu.VMEM((TAIL, half, PAIR), f32),
            dma((n_pairs,)), dma((4,)), dma((n_pairs,)),
            dma((n_parts,)), dma((n_parts,)), dma((n_parts,)), dma((n_parts,)),
            dma((n_parts,)), dma((n_parts,)),
            dma((n_cols,)), dma((n_cols,)),
            dma((TAIL, n_cols)), dma((TAIL, n_cols)), dma((TAIL,)), dma((TAIL,)),
        ],
        compiler_params=pltpu.CompilerParams(
            collective_id=0, has_side_effects=True, vmem_limit_bytes=60 * 1024 * 1024),
        cost_estimate=pl.CostEstimate(
            flops=2 * rows * feats * dout, bytes_accessed=feats * dout * 2, transcendentals=0),
    )(queries, keys, values, feat_weight, gain, out_weight)


def solution(mesh):
    return jax.shard_map(
        functools.partial(body, mesh.shape["seq"]),
        mesh=mesh,
        in_specs=(
            P(("groups", "seq"), "mp"),
            P(("groups", "seq"), "mp"),
            P(("groups", "seq"), "mp"),
            P("mp", None, None),
            P("mp"),
            P("mp", None),
        ),
        out_specs=P(("groups", "seq", "mp"), None),
        check_vma=False,
    )
```

```python
import functools

import jax
import jax.numpy as jnp
from jax import lax
from jax.experimental import pallas as pl
from jax.experimental.pallas import tpu as pltpu
from jax.sharding import PartitionSpec as P

HD = 128
PAIR = 2 * HD
COLS = 512
CUTS = 1
TAIL = 2
AHEAD = 2
MORE = 2
PART = HD // CUTS
MESH = pl.DeviceIdType.MESH
NT = (((1,), (1,)), ((), ()))


def feature(mapped):
    return jnp.where(mapped > 0.0, mapped + 1.0, jnp.exp(jnp.minimum(mapped, 0.0))).astype(jnp.bfloat16)


def kernel(
    n_seq, q_hbm, k_hbm, v_hbm, fw_hbm, gain_hbm, w_hbm, out_ref,
    q_buf, k_buf, v_buf, fw_buf, gain_buf, w_buf,
    vt_buf, fk_buf, intra_buf, nrm_buf, acc,
    s_buf, peer_s, p_buf, fwd, pre_out, pfx, mp_recv,
    stage, w_far, n_out, n_in,
    q_sem, kv_sem, w_sem,
    y_send, y_recv, z_send, z_recv, b_send, b_recv, mp_send, mp_recv_sem,
    wx_send, wx_recv, n_send, n_recv,
):
    grp = lax.axis_index("groups")
    me = lax.axis_index("seq")
    mp = lax.axis_index("mp")
    layer = lax.div(me, 2)
    side = lax.rem(me, 2)
    mate = (grp, me + 1 - 2 * side, mp)
    up = (grp, me + 2, mp)
    down = (grp, me - 2, mp)
    other_mp = 1 - mp
    peer = (grp, me, other_mp)
    has_down = layer > 0
    has_up = me + 2 < n_seq
    bottom = jnp.logical_not(has_down)
    top = jnp.logical_not(has_up)
    y_out = jnp.logical_or(side == 0, has_up)
    y_in = jnp.logical_or(side == 1, has_up)
    b_out = jnp.logical_or(side == 0, has_down)
    b_in = jnp.logical_or(side == 1, has_down)
    n_pairs = q_buf.shape[0]
    rows = q_buf.shape[1]
    half = rows // 2
    n_cols = acc.shape[0]
    n_kv = k_buf.shape[1] // HD
    pairs_kv = n_pairs // n_kv
    own_pairs = n_pairs // 2
    own_heads = 2 * own_pairs
    n_parts = own_heads * CUTS
    n_head = n_pairs - TAIL
    own_at = side * own_pairs
    mate_at = own_pairs - own_at

    def k_copy():
        return pltpu.make_async_copy(k_hbm, k_buf, kv_sem.at[0])

    def v_copy():
        return pltpu.make_async_copy(v_hbm, v_buf, kv_sem.at[1])

    def fw_copy():
        return pltpu.make_async_copy(fw_hbm, fw_buf, kv_sem.at[2])

    def gain_copy():
        return pltpu.make_async_copy(gain_hbm, gain_buf, kv_sem.at[3])

    def q_copy(i):
        at = pl.multiple_of(i * PAIR, PAIR)
        return pltpu.make_async_copy(q_hbm.at[:, pl.ds(at, PAIR)], q_buf.at[i], q_sem.at[i])

    def pair_of(j):
        return lax.rem(own_at + j, n_pairs)

    def w_copy(j):
        at = pl.multiple_of(pair_of(j) * PAIR, PAIR)
        to = pl.multiple_of(j * PAIR, PAIR)
        return pltpu.make_async_copy(w_hbm.at[pl.ds(at, PAIR), :], w_buf.at[pl.ds(to, PAIR), :], w_sem.at[j])

    def remote(src, dst, send, recv, device):
        return pltpu.make_async_remote_copy(
            src_ref=src, dst_ref=dst, send_sem=send, recv_sem=recv, device_id=device, device_id_type=MESH)

    def y_copy(k):
        return remote(s_buf.at[2 * CUTS * mate_at + k], peer_s.at[k], y_send.at[k], y_recv.at[k], mate)

    def z_copy(k):
        return remote(fwd.at[k], p_buf.at[k], z_send.at[k], z_recv.at[k], up)

    def b_copy(k):
        return remote(pre_out.at[k], pfx.at[n_parts + k], b_send.at[k], b_recv.at[k], mate)

    def mp_copy(c):
        return remote(
            acc.at[c], mp_recv.at[c],
            mp_send.at[c], mp_recv_sem.at[c], peer)

    def wx_copy(t, c):
        return remote(stage.at[t, c], w_far.at[t, c], wx_send.at[t, c], wx_recv.at[t, c], peer)

    def n_copy(t):
        return remote(n_out.at[t], n_in.at[t], n_send.at[t], n_recv.at[t], peer)

    k_copy().start()
    fw_copy().start()
    v_copy().start()

    barrier = pltpu.get_barrier_semaphore()
    pl.semaphore_signal(barrier, inc=1, device_id=mate, device_id_type=MESH)
    pl.semaphore_signal(barrier, inc=1, device_id=peer, device_id_type=MESH)

    @pl.when(has_up)
    def _():
        pl.semaphore_signal(barrier, inc=1, device_id=up, device_id_type=MESH)

    @pl.when(has_down)
    def _():
        pl.semaphore_signal(barrier, inc=1, device_id=down, device_id_type=MESH)

    gain_copy().start()

    for t in range(TAIL):
        w_copy(n_head + t).start()
    for t in range(2):
        q_copy(pair_of(t)).start()

    @pl.loop(2, n_pairs)
    def _(t):
        q_copy(pair_of(t)).start()

    @pl.loop(0, n_head)
    def _(t):
        w_copy(t).start()

    @pl.when(bottom)
    def _():
        p_buf[...] = jnp.zeros_like(p_buf)

    @pl.when(jnp.logical_not(b_in))
    def _():
        pfx[n_parts:] = jnp.zeros((n_parts, PART, HD), jnp.float32)

    k_copy().wait()
    fw_copy().wait()
    v_copy().wait()

    for g in range(n_kv):
        vt_buf[g] = v_buf[:, g * HD:(g + 1) * HD].T

    def states(i):
        kv_at = pl.multiple_of(lax.div(i, pairs_kv) * HD, HD)
        weight = jnp.concatenate([fw_buf[2 * i], fw_buf[2 * i + 1]], axis=1)
        fk = feature(jnp.dot(k_buf[:, pl.ds(kv_at, HD)], weight, preferred_element_type=jnp.float32))
        fk_buf[i] = fk
        state = jnp.dot(vt_buf[lax.div(i, pairs_kv)], fk, preferred_element_type=jnp.float32)
        for d in range(2):
            s_buf[pl.ds((2 * i + d) * CUTS, CUTS)] = state[:, d * HD:(d + 1) * HD].reshape(CUTS, PART, HD)

    @pl.loop(0, n_pairs, unroll=8)
    def _(t):
        states(lax.rem(mate_at + t, n_pairs))

    cols_step = n_cols // 4
    soon = 2

    def stage_cols(u):
        for d in range(cols_step):
            c = u * cols_step + d
            cols = pl.ds(pl.multiple_of(c * COLS, COLS), COLS)
            for t in range(TAIL):
                stage[t, c] = w_buf[pl.ds((n_head + t) * PAIR, PAIR), cols].astype(jnp.float32)

    def send_cols(u):
        for d in range(cols_step):
            for t in range(TAIL):
                wx_copy(t, u * cols_step + d).start()

    for t in range(TAIL):
        w_copy(n_head + t).wait()

    @pl.loop(0, soon)
    def _(u):
        stage_cols(u)

    pl.semaphore_wait(barrier, 2 + has_up.astype(jnp.int32) + has_down.astype(jnp.int32))

    @pl.when(y_out)
    def _():
        @pl.loop(0, n_parts)
        def _(k):
            y_copy(k).start()

    @pl.loop(0, soon)
    def _(u):
        send_cols(u)

    gain_copy().wait()

    def intra(i):
        zero = jnp.zeros((HD, HD), jnp.bfloat16)
        weight = jnp.concatenate(
            [jnp.concatenate([fw_buf[2 * i], zero], axis=1),
             jnp.concatenate([zero, fw_buf[2 * i + 1]], axis=1)], axis=0)
        fq = feature(jnp.dot(q_buf[i], weight, preferred_element_type=jnp.float32))
        q_buf[i] = fq
        kv_at = pl.multiple_of(lax.div(i, pairs_kv) * HD, HD)
        values = v_buf[:, pl.ds(kv_at, HD)]
        causal = (lax.broadcasted_iota(jnp.int32, (half, half), 0)
                  >= lax.broadcasted_iota(jnp.int32, (half, half), 1))
        for j in range(2):
            lanes = slice(j * HD, (j + 1) * HD)
            fk_h = fk_buf[i, :, lanes]
            fq_h = fq[:, lanes]
            first = lax.dot_general(fq_h[:half], fk_h[:half], NT, preferred_element_type=jnp.float32)
            first = jnp.where(causal, first, 0.0).astype(jnp.bfloat16)
            intra_buf[i, :half, lanes] = jnp.dot(first, values[:half], preferred_element_type=jnp.float32)
            left = lax.dot_general(fq_h[half:], fk_h[:half], NT, preferred_element_type=jnp.float32)
            right = lax.dot_general(fq_h[half:], fk_h[half:], NT, preferred_element_type=jnp.float32)
            right = jnp.where(causal, right, 0.0)
            low = jnp.concatenate([left.astype(jnp.bfloat16), right.astype(jnp.bfloat16)], axis=1)
            intra_buf[i, half:, lanes] = jnp.dot(low, values, preferred_element_type=jnp.float32)

    def serve(k):
        @pl.when(y_in)
        def _():
            y_copy(k).wait_recv()

        @pl.when(has_down)
        def _():
            z_copy(k).wait_recv()

        @pl.when(has_up)
        def _():
            fwd[k] = p_buf[k] + s_buf[2 * CUTS * own_at + k] + peer_s[k]
            z_copy(k).start()

        @pl.when(b_out)
        def _():
            pre_out[k] = p_buf[k] + jnp.where(side == 0, s_buf[2 * CUTS * own_at + k], 0.0)
            b_copy(k).start()

        pfx[k] = p_buf[k] + jnp.where(side == 1, peer_s[k], 0.0)

    def serve_head(h):
        for d in range(CUTS):
            serve(h * CUTS + d)

    second = layer == 1
    first_due = jnp.where(bottom, 3, jnp.where(second, 7, n_pairs))
    served = n_pairs - first_due
    @pl.loop(0, n_pairs)
    def _(u):
        @pl.when(u >= first_due)
        def _():
            serve_head(u - first_due)

        i = pair_of(u)
        q_copy(i).wait()
        intra(i)
        acc[u] = jnp.zeros((half, COLS), jnp.float32)

    @pl.when(layer >= 2)
    def _():
        @pl.loop(soon, 4)
        def _(u):
            stage_cols(u)
            send_cols(u)

    theirs = pl.ds(pl.multiple_of(other_mp * half, half), half)
    mine = pl.ds(pl.multiple_of(mp * half, half), half)

    def normed(j, span):
        i = pair_of(j)
        parts = []
        for d in range(2):
            lanes = slice(d * HD, (d + 1) * HD)
            prefix = pfx[pl.ds((2 * j + d) * CUTS, CUTS)].reshape(HD, HD)
            high = prefix.astype(jnp.bfloat16)
            low = (prefix - high.astype(jnp.float32)).astype(jnp.bfloat16)
            fq_h = q_buf[i, span, lanes]
            inter = lax.dot_general(
                jnp.concatenate([fq_h, fq_h], axis=1),
                jnp.concatenate([high, low], axis=1),
                NT, preferred_element_type=jnp.float32)
            attn = inter + intra_buf[i, span, lanes]
            scale = lax.rsqrt(jnp.mean(attn * attn, axis=-1, keepdims=True) + 1e-06)
            gain = gain_buf[pl.ds(2 * i + d, 1), :]
            parts.append((attn * scale * gain).astype(jnp.bfloat16))
        return jnp.concatenate(parts, axis=1)

    def mate_prefix(j):
        for d in range(2 * CUTS):
            b_copy((2 * j - own_heads) * CUTS + d).wait_recv()

    def attend(j):
        @pl.when(jnp.logical_and(j >= own_pairs, b_in))
        def _():
            mate_prefix(j)

        w_copy(j).wait()
        at = pl.multiple_of(j * PAIR, PAIR)
        sent = normed(j, theirs)
        for c in range(n_cols):
            acc[c] += jnp.dot(
                sent, w_buf[pl.ds(at, PAIR), c * COLS:(c + 1) * COLS], preferred_element_type=jnp.float32)
        nrm_buf[:, pl.ds(at, PAIR)] = normed(j, mine)

    def attend_last(t):
        j = n_head + t

        @pl.when(b_in)
        def _():
            mate_prefix(j)

        n_out[t] = normed(j, theirs).astype(jnp.float32)
        n_copy(t).start()
        nrm_buf[:, j * PAIR:(j + 1) * PAIR] = normed(j, mine)

    @pl.loop(0, own_heads + own_pairs)
    def _(t):
        @pl.when(t == own_heads - has_down.astype(jnp.int32))
        def _():
            @pl.when(y_out)
            def _():
                @pl.loop(0, n_parts)
                def _(k):
                    y_copy(k).wait_send()

        @pl.when(jnp.logical_and(t < own_heads, t >= served))
        def _():
            serve_head(t)

        @pl.when(jnp.logical_and(layer < 2, jnp.logical_and(t >= 2, t < 6 - soon)))
        def _():
            stage_cols(t - 2 + soon)
            send_cols(t - 2 + soon)

        odd = lax.rem(t, 2) == 1
        turn = lax.div(t, 2)
        inside = t < own_heads
        mid = own_heads // 2
        j_low = jnp.where(inside, turn, t - own_pairs)
        go_low = jnp.logical_or(odd, t >= own_heads)
        j_top = jnp.where(inside, jnp.where(odd, turn, own_pairs + turn - lax.div(mid, 2)), t - own_pairs + lax.div(mid, 2))
        go_top = jnp.logical_or(odd, t >= mid)
        j_bottom = t - (own_heads - 2)
        j = jnp.where(bottom, j_bottom, jnp.where(top, j_top, j_low))
        go = jnp.where(bottom, j_bottom >= 0, jnp.where(top, go_top, go_low))
        go = jnp.logical_and(go, j < n_head)

        @pl.when(go)
        def _():
            attend(j)

    @pl.loop(0, AHEAD)
    def _(c):
        mp_copy(c).start()

    @pl.loop(0, n_cols)
    def _(c):
        for t in range(TAIL):
            wx_copy(t, c).wait_send()
            wx_copy(t, c).wait_recv()

    total = stage.at[0]
    deep = n_head * PAIR

    def own_rows(c):
        at = pl.multiple_of(c * COLS, COLS)
        total[c] = jnp.dot(nrm_buf[:, :deep], w_buf[:deep, pl.ds(at, COLS)], preferred_element_type=jnp.float32)

    gap = n_cols // TAIL
    for t in range(TAIL):
        attend_last(t)

        if t < TAIL - 1:
            @pl.loop(AHEAD, AHEAD + MORE)
            def _(c):
                mp_copy(c).start()

        if t == TAIL - 1:
            @pl.loop(AHEAD + MORE, n_cols)
            def _(c):
                mp_copy(c).start()

        @pl.loop(t * gap, (t + 1) * gap, unroll=4)
        def _(c):
            own_rows(c)

    for t in range(TAIL):
        n_copy(t).wait_recv()

    far = jnp.concatenate([n_in[t] for t in range(TAIL)], axis=1).astype(jnp.bfloat16)
    last = jnp.concatenate([nrm_buf[:, deep:], far], axis=1)

    @pl.loop(0, n_cols, unroll=8)
    def _(c):
        at = pl.multiple_of(c * COLS, COLS)
        weight = jnp.concatenate(
            [w_buf[deep:, pl.ds(at, COLS)]] + [w_far[t, c].astype(jnp.bfloat16) for t in range(TAIL)], axis=0)
        total[c] += jnp.dot(last, weight, preferred_element_type=jnp.float32)

    for t in range(TAIL):
        n_copy(t).wait_send()

    @pl.loop(0, n_parts)
    def _(k):
        @pl.when(b_out)
        def _():
            b_copy(k).wait_send()

        @pl.when(has_up)
        def _():
            z_copy(k).wait_send()

    @pl.loop(0, n_cols, unroll=4)
    def _(c):
        mp_copy(c).wait_recv()
        at = pl.multiple_of(c * COLS, COLS)
        out_ref[:, pl.ds(at, COLS)] = (total[c] + mp_recv[c]).astype(jnp.bfloat16)

    @pl.loop(0, n_cols)
    def _(c):
        mp_copy(c).wait_send()


def body(n_seq, queries, keys, values, feat_weight, head_gain, out_weight):
    rows, feats = queries.shape
    heads = feat_weight.shape[0]
    n_pairs = heads // 2
    n_parts = n_pairs * CUTS
    dout = out_weight.shape[1]
    n_cols = dout // COLS
    half = rows // 2
    bf, f32 = jnp.bfloat16, jnp.float32
    gain = head_gain.reshape(heads, HD)
    dma = pltpu.SemaphoreType.DMA
    return pl.pallas_call(
        functools.partial(kernel, n_seq),
        out_shape=pltpu.VMEM((half, dout), bf),
        in_specs=[pl.BlockSpec(memory_space=pl.ANY)] * 6,
        out_specs=pl.BlockSpec(memory_space=pltpu.VMEM),
        scratch_shapes=[
            pltpu.VMEM((n_pairs, rows, PAIR), bf),
            pltpu.VMEM(keys.shape, bf),
            pltpu.VMEM(values.shape, bf),
            pltpu.VMEM(feat_weight.shape, bf),
            pltpu.VMEM((heads, HD), f32),
            pltpu.VMEM((feats, dout), bf),
            pltpu.VMEM((keys.shape[1] // HD, HD, rows), bf),
            pltpu.VMEM((n_pairs, rows, PAIR), bf),
            pltpu.VMEM((n_pairs, rows, PAIR), f32),
            pltpu.VMEM((half, feats), bf),
            pltpu.VMEM((n_cols, half, COLS), f32),
            pltpu.VMEM((2 * n_parts, PART, HD), f32),
            pltpu.VMEM((n_parts, PART, HD), f32),
            pltpu.VMEM((n_parts, PART, HD), f32),
            pltpu.VMEM((n_parts, PART, HD), f32),
            pltpu.VMEM((n_parts, PART, HD), f32),
            pltpu.VMEM((2 * n_parts, PART, HD), f32),
            pltpu.VMEM((n_cols, half, COLS), f32),
            pltpu.VMEM((TAIL, n_cols, PAIR, COLS), f32),
            pltpu.VMEM((TAIL, n_cols, PAIR, COLS), f32),
            pltpu.VMEM((TAIL, half, PAIR), f32),
            pltpu.VMEM((TAIL, half, PAIR), f32),
            dma((n_pairs,)), dma((4,)), dma((n_pairs,)),
            dma((n_parts,)), dma((n_parts,)), dma((n_parts,)), dma((n_parts,)),
            dma((n_parts,)), dma((n_parts,)),
            dma((n_cols,)), dma((n_cols,)),
            dma((TAIL, n_cols)), dma((TAIL, n_cols)), dma((TAIL,)), dma((TAIL,)),
        ],
        compiler_params=pltpu.CompilerParams(
            collective_id=0, has_side_effects=True, vmem_limit_bytes=60 * 1024 * 1024),
        cost_estimate=pl.CostEstimate(
            flops=2 * rows * feats * dout, bytes_accessed=feats * dout * 2, transcendentals=0),
    )(queries, keys, values, feat_weight, gain, out_weight)


def solution(mesh):
    return jax.shard_map(
        functools.partial(body, mesh.shape["seq"]),
        mesh=mesh,
        in_specs=(
            P(("groups", "seq"), "mp"),
            P(("groups", "seq"), "mp"),
            P(("groups", "seq"), "mp"),
            P("mp", None, None),
            P("mp"),
            P("mp", None),
        ),
        out_specs=P(("groups", "seq", "mp"), None),
        check_vma=False,
    )
```
